32 devices in a mesh: aux: 4 (over y, core), pair: 8 (over z, x).
Axes of the slice: x: 2, y: 2, z: 4, core: 2. Of those that a mesh axis runs over, the one named last changes fastest.
Arguments:
- amplitudes: bfloat16 [16384, 512], P('pair', 'aux'), may hold values from -4 to 4
- coulomb: bfloat16 [16384, 512], P('pair'), may hold values from -12 to 12
- df_factors: bfloat16 [16384, 2048], P('pair', 'aux'), may hold values from -0.111328125 to 0.111328125
- thc_left: bfloat16 [512, 1536], P('pair', 'aux'), may hold values from -0.50390625 to 0.50390625
- thc_right: bfloat16 [512, 1536], P('pair', 'aux'), may hold values from -0.50390625 to 0.50390625
- occ_energy: float32 [32], P('pair'), may hold values from -2 to -0.5
- vir_energy: float32 [512], replicated, may hold values from 0.5 to 3
- pivot_energy: float32 [1], replicated, may hold values from -2 to -0.5
Outputs:
- updated: bfloat16 [16384, 512], P('pair', 'aux')
The draws below stay inside these ranges and needn't reach their ends.
All inputs are finite; a program needn't handle non-finite values.
Results may differ from the reference program's by a relative error of at most 0.0051.
Values may be sent and summed in bfloat16 or wider, within the bound.
No kernel may reach another device: no remote copies, remote signals or barrier semaphores. Data moves between devices by JAX's collectives and lax.ppermute only.
A program may use at most 64 MiB of HBM per device.

```python
import jax
import jax.numpy as jnp
from jax import lax

V = 512
NAUX = 2048
NTHC = 1536
ITERS = 2
OCC = 32
PAIRS = 16384
N_AUX = 4


def block_levels(rng, dims, cuts, smallest, high):
    factor_of, own = 1.0, jax.random.fold_in(rng, 6)
    for axis_at, parts in cuts:
        steps = jnp.exp(jax.random.uniform(jax.random.fold_in(own, axis_at), (parts,), jnp.float32, smallest / len(cuts), high / len(cuts)))
        factor_of = factor_of * jnp.repeat(steps, dims[axis_at] // parts).reshape([-1 if axis == axis_at else 1 for axis in range(len(dims))])
    return factor_of


def centred(own_key, shape, deviation, limit, pieces=(), held_as=jnp.bfloat16):
    gain = block_levels(own_key, shape, pieces, -0.22, 0.18) if pieces else 1.0
    entries = jax.random.normal(own_key, shape, jnp.float32) * deviation * gain
    return jnp.minimum(jnp.maximum(entries, -limit), limit).astype(held_as)


def setup_inputs(seed: int = 0) -> dict:
    key_of = jax.random.split(jax.random.key(seed), 9)
    amplitudes = centred(key_of[0], (PAIRS, V), 0.5, 4.0, ((0, 8), (1, 4)))
    coulomb = centred(key_of[1], (PAIRS, V), 2.0, 12.0, ((0, 8),))
    df_factors = centred(key_of[2], (PAIRS, NAUX), ((2.0 / (NAUX * PAIRS) ** 0.5) ** 0.5), 0.111328125, ((0, 8), (1, 4)))
    thc_left = centred(key_of[3], (V, NTHC), ((V * NTHC ** 0.5) ** -0.25), 0.50390625, ((0, 8), (1, 4)))
    thc_right = centred(key_of[4], (V, NTHC), ((V * NTHC ** 0.5) ** -0.25), 0.50390625, ((0, 8), (1, 4)))
    occ_energy = jnp.clip(-2.0 + 1.5 * jax.random.uniform(key_of[5], (OCC,), jnp.float32) ** block_levels(key_of[5], (OCC,), ((0, 8),), -0.2, 0.2), -2.0, -0.5)
    vir_energy = jnp.clip(jax.random.uniform(key_of[6], (V,), jnp.float32, 0.5, 3.0), 0.5, 3.0)
    pivot_energy = jnp.clip(jax.random.uniform(key_of[7], (1,), jnp.float32, -2.0, -0.5), -2.0, -0.5)
    return dict(amplitudes=amplitudes, coulomb=coulomb, df_factors=df_factors, thc_left=thc_left, thc_right=thc_right, occ_energy=occ_energy, vir_energy=vir_energy, pivot_energy=pivot_energy)


def reference(amplitudes, coulomb, df_factors, thc_left, thc_right, occ_energy, vir_energy, pivot_energy):
    denom = (vir_energy[None, :, None] + vir_energy[None, None, :] - occ_energy[:, None, None] - pivot_energy[0]).reshape(PAIRS, V)
    aux_block = NAUX // N_AUX
    rank_block = NTHC // N_AUX
    amps = amplitudes
    for step in range(ITERS):
        total = jnp.zeros((PAIRS, V), jnp.float32)
        for block in range(N_AUX):
            factor_k = df_factors[:, block * aux_block:(block + 1) * aux_block]
            gram = lax.dot_general(factor_k, amps, (((0,), (0,)), ((), ())), preferred_element_type=jnp.float32).astype(jnp.bfloat16)
            cycle = jnp.dot(factor_k, gram, preferred_element_type=jnp.float32)
            left_k = thc_left[:, block * rank_block:(block + 1) * rank_block]
            right_k = thc_right[:, block * rank_block:(block + 1) * rank_block]
            proj = jnp.dot(amps, right_k, preferred_element_type=jnp.float32).reshape(OCC, V, rank_block)
            middle = jnp.sum(proj * left_k.astype(jnp.float32)[None], axis=1)
            weighted = (left_k.astype(jnp.float32)[None] * middle[:, None, :]).astype(jnp.bfloat16).reshape(PAIRS, rank_block)
            ladder = lax.dot_general(weighted, right_k, (((1,), (1,)), ((), ())), preferred_element_type=jnp.float32)
            total = total + (cycle + ladder)
        amps = ((coulomb.astype(jnp.float32) + total) / denom).astype(jnp.bfloat16)
    return amps
```

```python
import jax
import jax.numpy as jnp
from jax import lax
from jax.sharding import PartitionSpec as P

ITERS = 2
BF = jnp.bfloat16
F32 = jnp.float32


def xor(n, s):
    return [(i, i ^ s) for i in range(n)]


def dot(a, b, ca, cb):
    return lax.dot_general(a, b, (((ca,), (cb,)), ((), ())), preferred_element_type=F32)


def take(a, start, size):
    return lax.dynamic_slice_in_dim(a, start, size, 0)


def put(a, block, start):
    return lax.dynamic_update_slice_in_dim(a, block, start, 0)


def all_reduce(v, n):
    me = lax.axis_index("pair")
    low, high = me % 2, me // 2
    m = n // 2
    half = v.shape[0] // 2
    part = half // m

    def send(a, s):
        return lax.ppermute(a, "pair", xor(n, s))

    acc = take(v, low * half, half) + send(
        take(v, (1 - low) * half, half).astype(BF), 1
    ).astype(F32)
    rounded = acc.astype(BF)
    total = take(acc, high * part, part)
    for s in range(1, m):
        total = total + send(take(rounded, (high ^ s) * part, part), 2 * s).astype(F32)
    mine = total.astype(BF)
    line = put(jnp.zeros((half, v.shape[1]), BF), mine, high * part)
    for s in range(1, m):
        line = put(line, send(mine, 2 * s), (high ^ s) * part)
    other = send(line, 1)
    whole = put(jnp.zeros(v.shape, BF), line, low * half)
    return put(whole, other, (1 - low) * half)


def per_device(
    amplitudes, coulomb, df_factors, thc_left, thc_right, occ_energy, vir_energy, pivot_energy
):
    n_pair = lax.axis_size("pair")
    n_aux = lax.axis_size("aux")
    k = lax.axis_index("aux")
    me = lax.axis_index("pair")
    rows, width = amplitudes.shape
    nvirt = vir_energy.shape[0]
    nocc = rows // nvirt
    naux = df_factors.shape[1]

    def over(a, s):
        return lax.ppermute(a, "aux", xor(n_aux, s))

    amps = [amplitudes, over(amplitudes, 1), over(amplitudes, 2)]
    amps.append(over(amps[2], 1))

    fac = jnp.stack([thc_left, thc_right])
    fac = jnp.concatenate([fac, over(fac, 2)], axis=2)
    step, axis = n_pair // 2, 0
    while step:
        got = lax.ppermute(fac, "pair", xor(n_pair, step))
        first = (me // step) % 2 == 0
        fac = jnp.stack([jnp.where(first, fac, got), jnp.where(first, got, fac)], axis=axis)
        step, axis = step // 2, axis + 1
    cols = fac.shape[-1]
    fac = fac.reshape(n_pair, 2, -1, cols)
    left_half = fac[:, 0].reshape(nvirt, cols)
    right_half = fac[:, 1].reshape(nvirt, cols)
    sent = jnp.concatenate([left_half, take(right_half, (k ^ 1) * width, width)], axis=0)
    got = over(sent, 1)
    left = jnp.concatenate([left_half, got[:nvirt]], axis=1)
    right = jnp.concatenate([take(right_half, k * width, width), got[nvirt:]], axis=1)

    own = [df_factors[i * nvirt : (i + 1) * nvirt] for i in range(nocc)]
    core = over(df_factors, 1)
    core = [core[i * nvirt : (i + 1) * nvirt] for i in range(nocc)]
    far = [over(a, 2) for a in own]
    far_core = [over(a, 1) for a in far]
    factors = [list(blocks) for blocks in zip(own, core, far, far_core)]

    gram = jnp.concatenate([dot(df_factors, t, 0, 0) for t in amps], axis=0)
    gram = all_reduce(gram, n_pair)
    blocks = [gram[r * naux : (r + 1) * naux] for r in range(n_aux)]
    blocks = [blocks[0]] + [over(blocks[r], r) for r in range(1, n_aux)]

    t = [amplitudes[i * nvirt : (i + 1) * nvirt] for i in range(nocc)]
    vir_block = lax.dynamic_slice_in_dim(vir_energy, k * width, width, 0)
    coulomb_block = lax.dynamic_slice_in_dim(coulomb, k * width, width, 1)
    for step in range(ITERS):
        if step:
            gram = jnp.concatenate(
                [
                    sum(dot(factors[i][r], t[i], 0, 0) for i in range(nocc))
                    for r in range(n_aux)
                ],
                axis=0,
            )
            gram = all_reduce(gram, n_pair)
            blocks = [gram[r * naux : (r + 1) * naux] for r in range(n_aux)]
        middle = jnp.stack(
            [jnp.sum(dot(a, left, 0, 0) * right.astype(F32), axis=0) for a in t]
        )
        other = over(middle, 1)
        middle = middle + jnp.concatenate([other[:, cols:], other[:, :cols]], axis=1)
        other = over(middle, 2).reshape(nocc, 2, 2, cols // 2)
        middle = middle + other[:, :, ::-1].reshape(nocc, 2 * cols)
        new = []
        for i in range(nocc):
            scaled = (right.astype(F32) * middle[i][None, :]).astype(BF)
            res = dot(left, scaled, 1, 1)
            for r in range(n_aux):
                res = res + dot(factors[i][r], blocks[r], 1, 0)
            denom = (
                vir_energy[:, None] + vir_block[None, :] - occ_energy[i] - pivot_energy[0]
            )
            base = coulomb_block[i * nvirt : (i + 1) * nvirt].astype(F32)
            new.append(((base + res) / denom).astype(BF))
        t = new
    return jnp.concatenate(t, axis=0)


def solution(mesh):
    in_specs = (
        P("pair", "aux"),
        P("pair", None),
        P("pair", "aux"),
        P("pair", "aux"),
        P("pair", "aux"),
        P("pair"),
        P(),
        P(),
    )
    out_specs = P("pair", "aux")
    return jax.shard_map(
        per_device, mesh=mesh, in_specs=in_specs, out_specs=out_specs, check_vma=False
    )
```

```python
import functools

import jax
import jax.numpy as jnp
from jax import lax
from jax.experimental import pallas as pl
from jax.experimental.pallas import tpu as pltpu
from jax.sharding import PartitionSpec as P

ITERS = 2
BF = jnp.bfloat16
F32 = jnp.float32
VMEM = pl.BlockSpec(memory_space=pltpu.VMEM)
SMEM = pl.BlockSpec(memory_space=pltpu.SMEM)
PARAMS = pltpu.CompilerParams(vmem_limit_bytes=24 * 2**20)


def xor(n, s):
    return [(i, i ^ s) for i in range(n)]


def dot(a, b, ca, cb):
    return lax.dot_general(a, b, (((ca,), (cb,)), ((), ())), preferred_element_type=F32)


def take(a, start, size, axis=0):
    return lax.dynamic_slice_in_dim(a, start, size, axis)


def tie(a, *others):
    return lax.optimization_barrier((a, *others))


def all_reduce(v, n, cross=None, beside=lambda stage, a: a):
    me = lax.axis_index("pair")
    low, high = me % 2, me // 2
    m = n // 2
    half = v.shape[1] // 2
    part = half // m

    def send(a, s):
        return lax.ppermute(a, "pair", xor(n, s))

    got = beside(0, send(take(v, (1 - low) * half, half, 1).astype(BF), 1))
    acc = take(v, low * half, half, 1) + got.astype(F32)
    rounded = acc.astype(BF)
    total = take(acc, high * part, part, 1)
    for s in range(1, m):
        total = total + send(take(rounded, (high ^ s) * part, part, 1), 2 * s).astype(F32)
    mine = beside(1, total.astype(BF))
    if cross is not None:
        mine = beside(2, cross(mine))
    parts = [mine] + [send(mine, 2 * s) for s in range(1, m)]
    line = []
    for q in range(m):
        block = parts[0]
        for s in range(1, m):
            block = jnp.where((high ^ s) == q, parts[s], block)
        line.append(block)
    line = beside(3, jnp.concatenate(line, axis=1))
    return line, beside(4, send(line, 1))


def pieces(far):
    start = 0
    for block in far:
        yield start, block
        start += block.shape[0]


def residual_kernel(nfar, side, middle, left, right, line, other, own, *refs):
    far, (mine, theirs, gram) = refs[:nfar], refs[nfar:]
    nvirt, half, width = left.shape[0], line.shape[1], mine.shape[1]
    gram[:, pl.ds(pl.multiple_of(side[0] * half, half), half)] = line[...]
    gram[:, pl.ds(pl.multiple_of((1 - side[0]) * half, half), half)] = other[...]
    last = None
    for start, block in pieces(far):
        size = block.shape[0]
        i, at = start // nvirt, start % nvirt
        if i != last:
            scaled = (right[...].astype(F32) * middle[i : i + 1, :]).astype(BF)
            last = i
        res = dot(left[at : at + size], scaled, 1, 1)
        res += dot(own[start : start + size], gram[0], 1, 1)
        res += dot(block[...], gram[1], 1, 1)
        mine[start : start + size] = res[:, :width]
        theirs[start : start + size] = res[:, width:].astype(BF)


def update_kernel(last, occ, pivot, mine, got, coulomb, vir_col, vir_row, out):
    nvirt = vir_col.shape[0]
    for i in range(mine.shape[0] // nvirt):
        rows = slice(i * nvirt, (i + 1) * nvirt)
        denom = vir_col[...] + vir_row[...] - occ[i] - pivot[0]
        res = mine[rows] + got[rows].astype(F32)
        new = (coulomb[rows].astype(F32) + res) / denom
        if last:
            out[rows] = new.astype(BF)
        else:
            out[:, rows] = new.T.astype(BF)


def gram_kernel(nfar, mine, other, left, right, own, *refs):
    far, (gram, middle, amps) = refs[:nfar], refs[nfar:]
    width, nvirt = mine.shape[0], left.shape[0]
    amps[:width] = mine[...]
    amps[width:] = other[...]
    gram[0] = dot(amps[...], own[...], 1, 0)
    for start, block in pieces(far):
        term = dot(amps[:, start : start + block.shape[0]], block[...], 1, 0)
        if start:
            gram[1] += term
        else:
            gram[1] = term
    for i in range(middle.shape[0]):
        proj = dot(amps[:, i * nvirt : (i + 1) * nvirt], left[...], 1, 0)
        middle[i : i + 1] = jnp.sum(proj * right[...].astype(F32), axis=0, keepdims=True)


def per_device(
    amplitudes, coulomb, df_factors, thc_left, thc_right, occ_energy, vir_energy, pivot_energy
):
    n_pair = lax.axis_size("pair")
    n_aux = lax.axis_size("aux")
    k = lax.axis_index("aux")
    me = lax.axis_index("pair")
    rows, width = amplitudes.shape
    nvirt = vir_energy.shape[0]
    nocc = rows // nvirt
    naux = df_factors.shape[1]
    low = (me % 2).reshape(1)

    def over(a, s):
        return lax.ppermute(a, "aux", xor(n_aux, s))

    fac = jnp.stack([thc_left, thc_right])
    fac = jnp.concatenate([fac, over(fac, 2)], axis=2)
    cols = fac.shape[-1]

    def rows_over_pair(fac, axis):
        step = n_pair >> (axis + 1)
        got = lax.ppermute(fac, "pair", xor(n_pair, step))
        first = (me // step) % 2 == 0
        return jnp.stack([jnp.where(first, fac, got), jnp.where(first, got, fac)], axis=axis)

    n_steps = n_pair.bit_length() - 1

    flipped, fac = tie(amplitudes.T, fac)
    far_amps = over(flipped, 2)
    near = jnp.concatenate([flipped, over(flipped, 1)], axis=0)
    for axis in range(n_steps - 2):
        fac = rows_over_pair(fac, axis)
    far_amps, fac = tie(far_amps, fac)
    amps = jnp.concatenate([near, far_amps, over(far_amps, 1)], axis=0)

    n_far = 2 * nocc
    size = rows // n_far
    far = [over(df_factors[j * size : (j + 1) * size], 2) for j in range(n_far)]
    due = {0: (1,), 1: (2, 3), 2: (), 3: (4, 5), 4: (6, 7)}

    def beside(stage, a):
        nonlocal fac
        wanted = [j for j in due[stage] if j < n_far]
        a, *got = tie(a, *(far[j] for j in wanted))
        for j, b in zip(wanted, got):
            far[j] = b
        if stage == 0:
            a, fac = tie(a, rows_over_pair(fac, n_steps - 2))
        elif stage == 3:
            a, fac = tie(a, rows_over_pair(fac, n_steps - 1))
        return a

    gram = dot(amps, df_factors, 1, 0)
    gram, far[0] = tie(gram, far[0])
    gram = all_reduce(
        gram.reshape(2, -1, naux),
        n_pair,
        lambda a: jnp.stack([a[0], over(a[1], 2)]),
        beside,
    )

    fac = fac.reshape(n_pair, 2, -1, cols)
    left = fac[:, 0].reshape(nvirt, cols)
    right = fac[:, 1].reshape(nvirt, cols)
    right = jnp.concatenate(
        [take(right, k * width, width), take(right, (k ^ 1) * width, width)], axis=0
    )
    middle = jnp.stack(
        [
            jnp.sum(dot(near[:, i * nvirt : (i + 1) * nvirt], left, 1, 0) * right.astype(F32), axis=0)
            for i in range(nocc)
        ]
    )
    vir_col = vir_energy[:, None]
    vir_row = take(vir_energy, k * width, width)[None, :]
    coulomb_block = take(coulomb, k * width, width, 1)
    for step in range(ITERS):
        last = step == ITERS - 1
        other = over(middle, 2)
        middle = middle + jnp.concatenate([other[:, cols // 2 :], other[:, : cols // 2]], axis=1)
        mine, theirs = pl.pallas_call(
            functools.partial(residual_kernel, n_far),
            out_shape=(
                jax.ShapeDtypeStruct((rows, width), F32),
                jax.ShapeDtypeStruct((rows, width), BF),
            ),
            in_specs=[SMEM] + [VMEM] * (6 + n_far),
            out_specs=(VMEM, VMEM),
            scratch_shapes=[pltpu.VMEM((2, 2 * width, naux), BF)],
            compiler_params=PARAMS,
        )(low, middle, left, right, *gram, df_factors, *far)
        got = over(theirs, 1)
        new = pl.pallas_call(
            functools.partial(update_kernel, last),
            out_shape=jax.ShapeDtypeStruct((rows, width) if last else (width, rows), BF),
            in_specs=[SMEM] * 2 + [VMEM] * 5,
            out_specs=VMEM,
            compiler_params=PARAMS,
        )(occ_energy, pivot_energy, mine, got, coulomb_block, vir_col, vir_row)
        if not last:
            gram, middle = pl.pallas_call(
                functools.partial(gram_kernel, n_far),
                out_shape=(
                    jax.ShapeDtypeStruct((2, 2 * width, naux), F32),
                    jax.ShapeDtypeStruct((nocc, cols), F32),
                ),
                in_specs=[VMEM] * (5 + n_far),
                out_specs=(VMEM, VMEM),
                scratch_shapes=[pltpu.VMEM((2 * width, rows), BF)],
                compiler_params=PARAMS,
            )(new, over(new, 1), left, right, df_factors, *far)
            gram = all_reduce(gram, n_pair)
    return new


def solution(mesh):
    in_specs = (
        P("pair", "aux"),
        P("pair", None),
        P("pair", "aux"),
        P("pair", "aux"),
        P("pair", "aux"),
        P("pair"),
        P(),
        P(),
    )
    out_specs = P("pair", "aux")
    return jax.shard_map(
        per_device, mesh=mesh, in_specs=in_specs, out_specs=out_specs, check_vma=False
    )
```

```python
import functools

import jax
import jax.numpy as jnp
from jax import lax
from jax.experimental import pallas as pl
from jax.experimental.pallas import tpu as pltpu
from jax.sharding import PartitionSpec as P

ITERS = 2
BF = jnp.bfloat16
F32 = jnp.float32
VMEM = pl.BlockSpec(memory_space=pltpu.VMEM)
SMEM = pl.BlockSpec(memory_space=pltpu.SMEM)
FAR = lambda rows: [rows // 2, rows // 4, rows // 4]
DUE = {1: (0,), 3: (1,), 4: (2,)}
PARAMS = pltpu.CompilerParams(vmem_limit_bytes=12 * 2**20)


def xor(n, s):
    return [(i, i ^ s) for i in range(n)]


def dot(a, b, ca, cb):
    return lax.dot_general(a, b, (((ca,), (cb,)), ((), ())), preferred_element_type=F32)


def take(a, start, size, axis=0):
    return lax.dynamic_slice_in_dim(a, start, size, axis)


def tie(a, *others):
    return lax.optimization_barrier((a, *others))


def halves(v, low):
    half = v.shape[1] // 2
    return take(v, low * half, half, 1), take(v, (1 - low) * half, half, 1)


def fold(v, n):
    mine, theirs = halves(v, lax.axis_index("pair") % 2)
    return mine, lax.ppermute(theirs.astype(BF), "pair", xor(n, 1))


def all_reduce(mine, got, n, cross=None, beside=lambda stage, a: a):
    high = lax.axis_index("pair") // 2
    m = n // 2
    part = mine.shape[1] // m

    def send(a, s):
        return lax.ppermute(a, "pair", xor(n, s))

    acc = mine + beside(0, got).astype(F32)
    rounded = acc.astype(BF)
    total = take(acc, high * part, part, 1)
    for s in range(1, m):
        total = total + send(take(rounded, (high ^ s) * part, part, 1), 2 * s).astype(F32)
    mine = beside(1, total.astype(BF))
    if cross is not None:
        mine = beside(2, cross(mine))
    parts = [mine] + [send(mine, 2 * s) for s in range(1, m)]
    line = []
    for q in range(m):
        block = parts[0]
        for s in range(1, m):
            block = jnp.where((high ^ s) == q, parts[s], block)
        line.append(block)
    line = beside(3, jnp.concatenate(line, axis=1))
    return line, beside(4, send(line, 1))


def pieces(far, most):
    start = 0
    for block in far:
        at = 0
        while at < block.shape[0]:
            size = min(most - (start + at) % most, block.shape[0] - at)
            yield start + at, block[at : at + size]
            at += size
        start += at


def residual_kernel(nfar, side, middle, left, right, line, other, *refs):
    own, far, (mine, theirs, gram) = refs[0], refs[1 : 1 + nfar], refs[1 + nfar :]
    nvirt, half, width = left.shape[0], line.shape[1], mine.shape[1]
    gram[:, pl.ds(pl.multiple_of(side[0] * half, half), half)] = line[...]
    gram[:, pl.ds(pl.multiple_of((1 - side[0]) * half, half), half)] = other[...]
    last = None
    for start, block in pieces(far, nvirt):
        size = block.shape[0]
        i, at = start // nvirt, start % nvirt
        if i != last:
            scaled = (right[...].astype(F32) * middle[i : i + 1, :]).astype(BF)
            last = i
        res = dot(left[at : at + size], scaled, 1, 1)
        res += dot(own[start : start + size], gram[0], 1, 1)
        res += dot(block, gram[1], 1, 1)
        mine[start : start + size] = res[:, :width]
        theirs[start : start + size] = res[:, width:].astype(BF)


def update_kernel(last, occ, pivot, mine, got, coulomb, vir, vir_row, out):
    nvirt, width = vir.shape[1], mine.shape[1]
    virs = jnp.broadcast_to(vir[...], (width, nvirt)).T + vir_row[...]
    for i in range(mine.shape[0] // nvirt):
        rows = slice(i * nvirt, (i + 1) * nvirt)
        res = mine[rows] + got[rows].astype(F32)
        new = (coulomb[rows].astype(F32) + res) / (virs - occ[i] - pivot[0])
        if last:
            out[rows] = new.astype(BF)
        else:
            out[:, rows] = new.T.astype(BF)


def middle_kernel(mine, other, left, right, middle):
    width, nvirt = mine.shape[1], left.shape[0]
    for i in range(middle.shape[0]):
        total = None
        for at, amps in ((0, mine), (width, other)):
            proj = dot(amps[i * nvirt : (i + 1) * nvirt], left[...], 0, 0)
            term = jnp.sum(proj * right[at : at + width].astype(F32), axis=0, keepdims=True)
            total = term if total is None else total + term
        middle[i : i + 1] = total


def gram_kernel(nfar, mine, other, left, right, *refs):
    own, far, (gram, middle, amps) = refs[:1], refs[1 : 1 + nfar], refs[1 + nfar :]
    width, nvirt = mine.shape[0], left.shape[0]
    amps[:width] = mine[...]
    amps[width:] = other[...]
    for side, blocks in enumerate((own, far)):
        start = 0
        for block in blocks:
            term = dot(amps[:, start : start + block.shape[0]], block[...], 1, 0)
            gram[side] = gram[side] + term if start else term
            start += block.shape[0]
    for i in range(middle.shape[0]):
        proj = dot(amps[:, i * nvirt : (i + 1) * nvirt], left[...], 1, 0)
        middle[i : i + 1] = jnp.sum(proj * right[...].astype(F32), axis=0, keepdims=True)


def near_gram_kernel(mine, other, own, gram, *blocks):
    width = mine.shape[1]
    gram[:width] = dot(mine[...], own[...], 0, 0)
    gram[width:] = dot(other[...], own[...], 0, 0)
    start = 0
    for block in blocks:
        block[...] = own[start : start + block.shape[0]]
        start += block.shape[0]


def far_gram_kernel(mine, other, *refs):
    blocks, gram = refs[:-1], refs[-1]
    width = mine.shape[1]
    for at, amps in ((0, mine), (width, other)):
        start, total = 0, None
        for block in blocks:
            term = dot(amps[start : start + block.shape[0]], block[...], 0, 0)
            total = term if total is None else total + term
            start += block.shape[0]
        gram[at : at + width] = total


def per_device(
    amplitudes, coulomb, df_factors, thc_left, thc_right, occ_energy, vir_energy, pivot_energy
):
    n_pair = lax.axis_size("pair")
    n_aux = lax.axis_size("aux")
    k = lax.axis_index("aux")
    me = lax.axis_index("pair")
    rows, width = amplitudes.shape
    nvirt = vir_energy.shape[0]
    nocc = rows // nvirt
    naux = df_factors.shape[1]
    low = (me % 2).reshape(1)

    def over(a, s):
        return lax.ppermute(a, "aux", xor(n_aux, s))

    fac = jnp.stack([thc_left, thc_right])
    fac = jnp.concatenate([fac, over(fac, 2)], axis=2)
    cols = fac.shape[-1]

    def other_rows(fac, axis):
        bit = n_pair >> (axis + 1)
        got = lax.ppermute(fac, "pair", xor(n_pair, bit))
        first = (me // bit) % 2 == 0
        return jnp.where(first, fac, got), jnp.where(first, got, fac)

    n_bits = n_pair.bit_length() - 1

    far_amps = over(amplitudes, 2)
    near = [amplitudes, over(amplitudes, 1)]

    sizes = FAR(rows)
    n_far = len(sizes)
    gram_shape = jax.ShapeDtypeStruct((2 * width, naux), F32)

    gram, *own = pl.pallas_call(
        near_gram_kernel,
        out_shape=(gram_shape, *(jax.ShapeDtypeStruct((size, naux), BF) for size in sizes)),
        in_specs=[VMEM] * 3,
        out_specs=(VMEM,) * (1 + n_far),
        compiler_params=PARAMS,
    )(*near, df_factors)
    near_mine, near_got = fold(gram[None], n_pair)
    far_amps, near_got, fac = tie(far_amps, near_got, fac)
    far_other = over(far_amps, 1)
    far_other, fac = tie(far_other, fac)
    gram = pl.pallas_call(
        far_gram_kernel,
        out_shape=gram_shape,
        in_specs=[VMEM] * (2 + n_far),
        out_specs=VMEM,
        compiler_params=PARAMS,
    )(far_amps, far_other, *own)
    far_mine, far_got = fold(gram[None], n_pair)

    far = [over(block, 2) for block in own]

    vir = vir_energy[None, :]
    vir_row = take(vir_energy, k * width, width)[None, :]
    coulomb_block = take(coulomb, k * width, width, 1)

    def beside(stage, a):
        nonlocal fac, vir, vir_row, coulomb_block
        a, *got = tie(a, *(far[j] for j in DUE.get(stage, ())))
        for j, b in zip(DUE.get(stage, ()), got):
            far[j] = b
        if stage == 1:
            one, two = other_rows(fac, 0)
            kept = jnp.where(k // 2 == 0, one[1], two[1])
            fac = jnp.stack([one[0], two[0], kept])[:, None]
            a, vir, vir_row, coulomb_block = tie(a, vir, vir_row, coulomb_block)
        elif stage == 2:
            for axis in range(n_bits - 2, 0, -1):
                fac = jnp.stack(other_rows(fac, axis), axis=1)
                fac = fac.reshape(3, -1, *fac.shape[3:])
            a, fac = tie(a, fac)
        elif stage == 3:
            fac = jnp.stack(other_rows(fac, n_bits - 1), axis=2).reshape(3, -1, *fac.shape[2:])
            a, fac = tie(a, fac)
        return a

    gram = all_reduce(
        jnp.concatenate([near_mine, far_mine], axis=0),
        jnp.concatenate([near_got, beside(5, far_got)], axis=0),
        n_pair,
        lambda a: jnp.stack([a[0], over(a[1], 2)]),
        beside,
    )

    left = fac[:2].reshape(nvirt, cols)
    right = fac[2].reshape(2, width, cols)
    right = jnp.where(k % 2 == 0, right, right[::-1]).reshape(2 * width, cols)
    middle = pl.pallas_call(
        middle_kernel,
        out_shape=jax.ShapeDtypeStruct((nocc, cols), F32),
        in_specs=[VMEM] * 4,
        out_specs=VMEM,
        compiler_params=PARAMS,
    )(*near, left, right)
    for step in range(ITERS):
        last = step == ITERS - 1
        other = over(middle, 2)
        middle = middle + jnp.concatenate([other[:, cols // 2 :], other[:, : cols // 2]], axis=1)
        mine, theirs = pl.pallas_call(
            functools.partial(residual_kernel, n_far),
            out_shape=(
                jax.ShapeDtypeStruct((rows, width), F32),
                jax.ShapeDtypeStruct((rows, width), BF),
            ),
            in_specs=[SMEM] + [VMEM] * (6 + n_far),
            out_specs=(VMEM, VMEM),
            scratch_shapes=[pltpu.VMEM((2, 2 * width, naux), BF)],
            compiler_params=PARAMS,
        )(low, middle, left, right, *gram, df_factors, *far)
        got = over(theirs, 1)
        new = pl.pallas_call(
            functools.partial(update_kernel, last),
            out_shape=jax.ShapeDtypeStruct((rows, width) if last else (width, rows), BF),
            in_specs=[SMEM] * 2 + [VMEM] * 5,
            out_specs=VMEM,
            compiler_params=PARAMS,
        )(occ_energy, pivot_energy, mine, got, coulomb_block, vir, vir_row)
        if not last:
            gram, middle = pl.pallas_call(
                functools.partial(gram_kernel, n_far),
                out_shape=(
                    jax.ShapeDtypeStruct((2, 2 * width, naux), F32),
                    jax.ShapeDtypeStruct((nocc, cols), F32),
                ),
                in_specs=[VMEM] * (5 + n_far),
                out_specs=(VMEM, VMEM),
                scratch_shapes=[pltpu.VMEM((2 * width, rows), BF)],
                compiler_params=PARAMS,
            )(new, over(new, 1), left, right, df_factors, *far)
            gram = all_reduce(*fold(gram, n_pair), n_pair)
    return new


def solution(mesh):
    in_specs = (
        P("pair", "aux"),
        P("pair", None),
        P("pair", "aux"),
        P("pair", "aux"),
        P("pair", "aux"),
        P("pair"),
        P(),
        P(),
    )
    out_specs = P("pair", "aux")
    return jax.shard_map(
        per_device, mesh=mesh, in_specs=in_specs, out_specs=out_specs, check_vma=False
    )
```

```python
import functools

import jax
import jax.numpy as jnp
from jax import lax
from jax.experimental import pallas as pl
from jax.experimental.pallas import tpu as pltpu
from jax.sharding import PartitionSpec as P

ITERS = 2
BF = jnp.bfloat16
F32 = jnp.float32
VMEM = pl.BlockSpec(memory_space=pltpu.VMEM)
SMEM = pl.BlockSpec(memory_space=pltpu.SMEM)
ANY = pl.BlockSpec(memory_space=pl.ANY)
FAR = lambda rows: [rows // 2, rows // 4, rows // 4]
DUE = {1: (0,), 3: (1,), 4: (2,)}
PARAMS = pltpu.CompilerParams(vmem_limit_bytes=12 * 2**20)


def xor(n, s):
    return [(i, i ^ s) for i in range(n)]


def dot(a, b, ca, cb):
    return lax.dot_general(a, b, (((ca,), (cb,)), ((), ())), preferred_element_type=F32)


def take(a, start, size, axis=0):
    return lax.dynamic_slice_in_dim(a, start, size, axis)


def tie(a, *others):
    return lax.optimization_barrier((a, *others))


def halves(v, low):
    half = v.shape[1] // 2
    return take(v, low * half, half, 1), take(v, (1 - low) * half, half, 1)


def fold(v, n):
    mine, theirs = halves(v, lax.axis_index("pair") % 2)
    return mine, lax.ppermute(theirs.astype(BF), "pair", xor(n, 1))


def all_reduce(mine, got, n, beside=lambda stage, a: a):
    high = lax.axis_index("pair") // 2
    m = n // 2
    part = mine.shape[1] // m

    def send(a, s):
        return lax.ppermute(a, "pair", xor(n, s))

    acc = mine + beside(0, got).astype(F32)
    rounded = acc.astype(BF)
    total = take(acc, high * part, part, 1)
    for s in range(1, m):
        total = total + send(take(rounded, (high ^ s) * part, part, 1), 2 * s).astype(F32)
    mine = beside(1, total.astype(BF))
    parts = [mine] + [send(mine, 2 * s) for s in range(1, m)]
    line = []
    for q in range(m):
        block = parts[0]
        for s in range(1, m):
            block = jnp.where((high ^ s) == q, parts[s], block)
        line.append(block)
    line = beside(2, jnp.concatenate(line, axis=1))
    return line, beside(3, send(line, 1))


def hold_kernel(own, far, out, sems):
    copies = [pltpu.make_async_copy(a, out.at[r], sems.at[r]) for r, a in enumerate((own, far))]
    for copy in copies:
        copy.start()
    for copy in copies:
        copy.wait()


def residual_kernel(swapped, side, middle, left, right, factors, line, other, *refs):
    mine, theirs, gram = refs[-3:]
    nvirt, half, width = left.shape[0], line.shape[1], mine.shape[1]
    near = (line, other)
    for j in range(2):
        rows = pl.ds(pl.multiple_of((side[0] if j == 0 else 1 - side[0]) * half, half), half)
        gram[0, rows] = near[j][0]
        gram[1, rows] = refs[0][j] if swapped else near[j][1]
    size = min(nvirt, 256)
    for start in range(0, mine.shape[0], size):
        i, at = start // nvirt, start % nvirt
        if at == 0:
            scaled = (right[...].astype(F32) * middle[i : i + 1, :]).astype(BF)
        rows = slice(start, start + size)
        res = dot(left[at : at + size], scaled, 1, 1)
        for r in range(2):
            res += dot(factors[r, rows], gram[r], 1, 1)
        mine[rows] = res[:, :width]
        theirs[rows] = res[:, width:].astype(BF)


def update_kernel(last, occ, pivot, mine, got, coulomb, vir, vir_row, out):
    nvirt, width = vir.shape[1], mine.shape[1]
    virs = jnp.broadcast_to(vir[...], (width, nvirt)).T + vir_row[...]
    for i in range(mine.shape[0] // nvirt):
        rows = slice(i * nvirt, (i + 1) * nvirt)
        res = mine[rows] + got[rows].astype(F32)
        new = (coulomb[rows].astype(F32) + res) / (virs - occ[i] - pivot[0])
        if last:
            out[rows] = new.astype(BF)
        else:
            out[:, rows] = new.T.astype(BF)


def middle_kernel(mine, other, left, right, middle):
    width, nvirt = mine.shape[1], left.shape[0]
    for i in range(middle.shape[0]):
        total = None
        for at, amps in ((0, mine), (width, other)):
            proj = dot(amps[i * nvirt : (i + 1) * nvirt], left[...], 0, 0)
            term = jnp.sum(proj * right[at : at + width].astype(F32), axis=0, keepdims=True)
            total = term if total is None else total + term
        middle[i : i + 1] = total


def gram_kernel(mine, other, left, right, factors, gram, middle, amps):
    width, nvirt = mine.shape[0], left.shape[0]
    amps[:width] = mine[...]
    amps[width:] = other[...]
    for r in range(2):
        gram[r] = dot(amps[...], factors[r], 1, 0)
    for i in range(middle.shape[0]):
        proj = dot(amps[:, i * nvirt : (i + 1) * nvirt], left[...], 1, 0)
        middle[i : i + 1] = jnp.sum(proj * right[...].astype(F32), axis=0, keepdims=True)


def first_gram_kernel(mine, other, own, gram):
    width = mine.shape[1]
    gram[:width] = dot(mine[...], own[...], 0, 0)
    gram[width:] = dot(other[...], own[...], 0, 0)


def per_device(
    amplitudes, coulomb, df_factors, thc_left, thc_right, occ_energy, vir_energy, pivot_energy
):
    n_pair = lax.axis_size("pair")
    n_aux = lax.axis_size("aux")
    k = lax.axis_index("aux")
    me = lax.axis_index("pair")
    rows, width = amplitudes.shape
    nvirt = vir_energy.shape[0]
    nocc = rows // nvirt
    naux = df_factors.shape[1]
    low = (me % 2).reshape(1)

    def over(a, s):
        return lax.ppermute(a, "aux", xor(n_aux, s))

    fac = jnp.stack([thc_left, thc_right])
    fac = jnp.concatenate([fac, over(fac, 2)], axis=2)
    cols = fac.shape[-1]

    def other_rows(fac, axis):
        bit = n_pair >> (axis + 1)
        got = lax.ppermute(fac, "pair", xor(n_pair, bit))
        first = (me // bit) % 2 == 0
        return jnp.where(first, fac, got), jnp.where(first, got, fac)

    n_bits = n_pair.bit_length() - 1

    far_amps = over(amplitudes, 2)
    near = [amplitudes, over(amplitudes, 1)]

    def first_gram(pair_of):
        return pl.pallas_call(
            first_gram_kernel,
            out_shape=jax.ShapeDtypeStruct((2 * width, naux), F32),
            in_specs=[VMEM] * 3,
            out_specs=VMEM,
            compiler_params=PARAMS,
        )(*pair_of, df_factors)[None]

    near_mine, near_got = fold(first_gram(near), n_pair)
    far_amps, near_got, fac = tie(far_amps, near_got, fac)
    far_other, fac = tie(over(far_amps, 1), fac)
    far_gram = first_gram([far_amps, far_other])

    one, two = other_rows(fac, 0)
    kept = jnp.where(k // 2 == 0, one[1], two[1])
    fac = jnp.stack([one[0], two[0], kept])[:, None]
    far_gram, fac = tie(far_gram, fac)
    far_mine, far_got = fold(far_gram, n_pair)

    far = over(df_factors, 2)
    vir = vir_energy[None, :]
    vir_row = take(vir_energy, k * width, width)[None, :]
    coulomb_block = take(coulomb, k * width, width, 1)

    left = right = middle = factors = None

    def beside(stage, a):
        nonlocal fac, far, vir, vir_row, coulomb_block, left, right, middle, factors
        if stage == 1:
            fac = jnp.stack(other_rows(fac, n_bits - 1), axis=2).reshape(3, 1, -1, *fac.shape[2:])
            a, fac = tie(a, fac)
        if stage == 1:
            a, vir, vir_row, coulomb_block = tie(a, vir, vir_row, coulomb_block)
        if stage == 4:
            for axis in range(n_bits - 2, 0, -1):
                fac = jnp.stack(other_rows(fac, axis), axis=1)
                fac = fac.reshape(3, -1, *fac.shape[3:])
            left = fac[:2].reshape(nvirt, cols)
            right = fac[2].reshape(2, width, cols)
            right = jnp.where(k % 2 == 0, right, right[::-1]).reshape(2 * width, cols)
            middle = pl.pallas_call(
                middle_kernel,
                out_shape=jax.ShapeDtypeStruct((nocc, cols), F32),
                in_specs=[VMEM] * 4,
                out_specs=VMEM,
                compiler_params=PARAMS,
            )(*near, left, right)
        if stage == 4:
            a, far = tie(a, far)
            factors = pl.pallas_call(
                hold_kernel,
                out_shape=jax.ShapeDtypeStruct((2, rows, naux), BF),
                in_specs=[ANY] * 2,
                out_specs=VMEM,
                scratch_shapes=[pltpu.SemaphoreType.DMA((2,))],
                compiler_params=PARAMS,
            )(df_factors, far)
        return a

    line, other = all_reduce(
        jnp.concatenate([near_mine, far_mine], axis=0),
        jnp.concatenate([near_got, far_got], axis=0),
        n_pair,
        beside,
    )
    swapped = beside(4, over(jnp.stack([line[1], other[1]]), 2))
    gram = (line, other, swapped)
    for step in range(ITERS):
        last = step == ITERS - 1
        other = over(middle, 2)
        middle = middle + jnp.concatenate([other[:, cols // 2 :], other[:, : cols // 2]], axis=1)
        mine, theirs = pl.pallas_call(
            functools.partial(residual_kernel, step == 0),
            out_shape=(
                jax.ShapeDtypeStruct((rows, width), F32),
                jax.ShapeDtypeStruct((rows, width), BF),
            ),
            in_specs=[SMEM] + [VMEM] * (4 + len(gram)),
            out_specs=(VMEM, VMEM),
            scratch_shapes=[pltpu.VMEM((2, 2 * width, naux), BF)],
            compiler_params=PARAMS,
        )(low, middle, left, right, factors, *gram)
        got = over(theirs, 1)
        new = pl.pallas_call(
            functools.partial(update_kernel, last),
            out_shape=jax.ShapeDtypeStruct((rows, width) if last else (width, rows), BF),
            in_specs=[SMEM] * 2 + [VMEM] * 5,
            out_specs=VMEM,
            compiler_params=PARAMS,
        )(occ_energy, pivot_energy, mine, got, coulomb_block, vir, vir_row)
        if not last:
            gram, middle = pl.pallas_call(
                gram_kernel,
                out_shape=(
                    jax.ShapeDtypeStruct((2, 2 * width, naux), F32),
                    jax.ShapeDtypeStruct((nocc, cols), F32),
                ),
                in_specs=[VMEM] * 5,
                out_specs=(VMEM, VMEM),
                scratch_shapes=[pltpu.VMEM((2 * width, rows), BF)],
                compiler_params=PARAMS,
            )(new, over(new, 1), left, right, factors)
            gram = all_reduce(*fold(gram, n_pair), n_pair)
    return new


def solution(mesh):
    in_specs = (
        P("pair", "aux"),
        P("pair", None),
        P("pair", "aux"),
        P("pair", "aux"),
        P("pair", "aux"),
        P("pair"),
        P(),
        P(),
    )
    out_specs = P("pair", "aux")
    return jax.shard_map(
        per_device, mesh=mesh, in_specs=in_specs, out_specs=out_specs, check_vma=False
    )
```

```python
import functools

import jax
import jax.numpy as jnp
from jax import lax
from jax.experimental import pallas as pl
from jax.experimental.pallas import tpu as pltpu
from jax.sharding import PartitionSpec as P

ITERS = 2
BF = jnp.bfloat16
F32 = jnp.float32
VMEM = pl.BlockSpec(memory_space=pltpu.VMEM)
SMEM = pl.BlockSpec(memory_space=pltpu.SMEM)
ANY = pl.BlockSpec(memory_space=pl.ANY)
FAR = lambda rows: [rows // 2, rows // 4, rows // 4]
DUE = {1: (0,), 3: (1,), 4: (2,)}
PARAMS = pltpu.CompilerParams(vmem_limit_bytes=12 * 2**20)


def xor(n, s):
    return [(i, i ^ s) for i in range(n)]


def dot(a, b, ca, cb):
    return lax.dot_general(a, b, (((ca,), (cb,)), ((), ())), preferred_element_type=F32)


def take(a, start, size, axis=0):
    return lax.dynamic_slice_in_dim(a, start, size, axis)


def tie(a, *others):
    return lax.optimization_barrier((a, *others))


def halves(v, low):
    half = v.shape[1] // 2
    return take(v, low * half, half, 1), take(v, (1 - low) * half, half, 1)


def fold(v, n):
    mine, theirs = halves(v, lax.axis_index("pair") % 2)
    return mine, lax.ppermute(theirs.astype(BF), "pair", xor(n, 1))


def all_reduce(mine, got, n, beside=lambda stage, a: a):
    high = lax.axis_index("pair") // 2
    m = n // 2
    part = mine.shape[1] // m

    def send(a, s):
        return lax.ppermute(a, "pair", xor(n, s))

    acc = mine + beside(0, got).astype(F32)
    rounded = acc.astype(BF)
    total = take(acc, high * part, part, 1)
    for s in range(1, m):
        total = total + send(take(rounded, (high ^ s) * part, part, 1), 2 * s).astype(F32)
    mine = beside(1, total.astype(BF))
    parts = [mine] + [send(mine, 2 * s) for s in range(1, m)]
    line = []
    for q in range(m):
        block = parts[0]
        for s in range(1, m):
            block = jnp.where((high ^ s) == q, parts[s], block)
        line.append(block)
    line = beside(2, jnp.concatenate(line, axis=1))
    return line, beside(3, send(line, 1))


def hold_kernel(own, far, out, sems):
    copies = [pltpu.make_async_copy(a, out.at[r], sems.at[r]) for r, a in enumerate((own, far))]
    for copy in copies:
        copy.start()
    for copy in copies:
        copy.wait()


def residual_kernel(swapped, side, middle, left, right, factors, one, two, mine, theirs, gram):
    nvirt, half, width = left.shape[0], one.shape[1], mine.shape[1]
    for j in range(2):
        rows = pl.ds(pl.multiple_of((side[0] if j == 0 else 1 - side[0]) * half, half), half)
        for r in range(2):
            gram[r, rows] = (one, two)[r][j] if swapped else (one, two)[j][r]
    size = min(nvirt, 256)
    for start in range(0, mine.shape[0], size):
        i, at = start // nvirt, start % nvirt
        if at == 0:
            scaled = (right[...].astype(F32) * middle[i : i + 1, :]).astype(BF)
        rows = slice(start, start + size)
        res = dot(left[at : at + size], scaled, 1, 1)
        for r in range(2):
            res += dot(factors[r, rows], gram[r], 1, 1)
        mine[rows] = res[:, :width]
        theirs[rows] = res[:, width:].astype(BF)


def update_kernel(last, occ, pivot, mine, got, coulomb, vir, vir_row, out):
    nvirt, width = vir.shape[1], mine.shape[1]
    virs = jnp.broadcast_to(vir[...], (width, nvirt)).T + vir_row[...]
    for i in range(mine.shape[0] // nvirt):
        rows = slice(i * nvirt, (i + 1) * nvirt)
        res = mine[rows] + got[rows].astype(F32)
        new = (coulomb[rows].astype(F32) + res) / (virs - occ[i] - pivot[0])
        if last:
            out[rows] = new.astype(BF)
        else:
            out[:, rows] = new.T.astype(BF)


def middle_kernel(mine, other, places, one, two, left, right, middle):
    width, nvirt = mine.shape[1], left.shape[0]
    part = one.shape[1]
    for a, at, column in ((one, places[0], places[1]), (two, 1 - places[0], 1 - places[1])):
        for top in range(2):
            left[pl.ds(pl.multiple_of(top * 2 * part + at * part, part), part)] = a[top]
        right[pl.ds(pl.multiple_of(column * part, part), part)] = a[2]
    for i in range(middle.shape[0]):
        total = None
        for at, amps in ((0, mine), (width, other)):
            proj = dot(amps[i * nvirt : (i + 1) * nvirt], left[...], 0, 0)
            term = jnp.sum(proj * right[at : at + width].astype(F32), axis=0, keepdims=True)
            total = term if total is None else total + term
        middle[i : i + 1] = total


def gram_kernel(mine, other, left, right, factors, gram, middle, amps):
    width, nvirt = mine.shape[0], left.shape[0]
    amps[:width] = mine[...]
    amps[width:] = other[...]
    for r in range(2):
        gram[r] = dot(amps[...], factors[r], 1, 0)
    for i in range(middle.shape[0]):
        proj = dot(amps[:, i * nvirt : (i + 1) * nvirt], left[...], 1, 0)
        middle[i : i + 1] = jnp.sum(proj * right[...].astype(F32), axis=0, keepdims=True)


def first_gram_kernel(mine, other, own, gram):
    width = mine.shape[1]
    gram[:width] = dot(mine[...], own[...], 0, 0)
    gram[width:] = dot(other[...], own[...], 0, 0)


def scheduled(micros):
    return pl.CostEstimate(flops=int(micros * 1e9), bytes_accessed=int(micros * 3e6), transcendentals=0)


def per_device(
    amplitudes, coulomb, df_factors, thc_left, thc_right, occ_energy, vir_energy, pivot_energy
):
    n_pair = lax.axis_size("pair")
    n_aux = lax.axis_size("aux")
    k = lax.axis_index("aux")
    me = lax.axis_index("pair")
    rows, width = amplitudes.shape
    nvirt = vir_energy.shape[0]
    nocc = rows // nvirt
    naux = df_factors.shape[1]
    low = (me % 2).reshape(1)

    def over(a, s):
        return lax.ppermute(a, "aux", xor(n_aux, s))

    fac = jnp.stack([thc_left, thc_right])
    fac = jnp.concatenate([fac, over(fac, 2)], axis=2)
    cols = fac.shape[-1]

    def other_rows(fac, axis):
        bit = n_pair >> (axis + 1)
        got = lax.ppermute(fac, "pair", xor(n_pair, bit))
        first = (me // bit) % 2 == 0
        return jnp.where(first, fac, got), jnp.where(first, got, fac)

    n_bits = n_pair.bit_length() - 1

    far_amps = over(amplitudes, 2)
    near = [amplitudes, over(amplitudes, 1)]

    def first_gram(pair_of):
        return pl.pallas_call(
            first_gram_kernel,
            out_shape=jax.ShapeDtypeStruct((2 * width, naux), F32),
            in_specs=[VMEM] * 3,
            out_specs=VMEM,
            compiler_params=PARAMS,
        )(*pair_of, df_factors)[None]

    near_mine, near_got = fold(first_gram(near), n_pair)
    far_amps, near_got, fac = tie(far_amps, near_got, fac)
    far_other, fac = tie(over(far_amps, 1), fac)
    far_gram = first_gram([far_amps, far_other])

    one, two = other_rows(fac, 0)
    kept = jnp.where(k // 2 == 0, one[1], two[1])
    fac = jnp.stack([one[0], two[0], kept])
    far_gram, fac = tie(far_gram, fac)
    far_mine, far_got = fold(far_gram, n_pair)

    far = over(df_factors, 2)
    vir = vir_energy[None, :]
    vir_row = take(vir_energy, k * width, width)[None, :]
    coulomb_block = take(coulomb, k * width, width, 1)

    left = right = middle = factors = None

    def beside(stage, a):
        nonlocal fac, far, vir, vir_row, coulomb_block, left, right, middle, factors
        if stage == 1:
            fac = jnp.concatenate(other_rows(fac, n_bits - 1), axis=1)
            a, fac = tie(a, fac)
        if stage == 1:
            a, vir, vir_row, coulomb_block = tie(a, vir, vir_row, coulomb_block)
        if stage == 4:
            for axis in range(n_bits - 2, 1, -1):
                fac = jnp.concatenate(other_rows(fac, axis), axis=1)
            got = lax.ppermute(fac, "pair", xor(n_pair, n_pair // 4))
            bit = (me >> (n_bits - 2)) % 2
            left, right, middle = pl.pallas_call(
                middle_kernel,
                out_shape=(
                    jax.ShapeDtypeStruct((nvirt, cols), BF),
                    jax.ShapeDtypeStruct((2 * width, cols), BF),
                    jax.ShapeDtypeStruct((nocc, cols), F32),
                ),
                in_specs=[VMEM] * 2 + [SMEM] + [VMEM] * 2,
                out_specs=(VMEM,) * 3,
                cost_estimate=scheduled(6),
                compiler_params=PARAMS,
            )(*near, jnp.stack([bit, bit ^ (k % 2)]), fac, got)
        if stage == 4:
            a, far = tie(a, far)
            factors = pl.pallas_call(
                hold_kernel,
                out_shape=jax.ShapeDtypeStruct((2, rows, naux), BF),
                in_specs=[ANY] * 2,
                out_specs=VMEM,
                scratch_shapes=[pltpu.SemaphoreType.DMA((2,))],
                compiler_params=PARAMS,
            )(df_factors, far)
        return a

    line, other = all_reduce(
        jnp.concatenate([near_mine, far_mine], axis=0),
        jnp.concatenate([near_got, far_got], axis=0),
        n_pair,
        beside,
    )
    gram = (jnp.stack([line[0], other[0]]), beside(4, over(jnp.stack([line[1], other[1]]), 2)))
    for step in range(ITERS):
        last = step == ITERS - 1
        other = over(middle, 2)
        middle = middle + jnp.concatenate([other[:, cols // 2 :], other[:, : cols // 2]], axis=1)
        mine, theirs = pl.pallas_call(
            functools.partial(residual_kernel, step == 0),
            out_shape=(
                jax.ShapeDtypeStruct((rows, width), F32),
                jax.ShapeDtypeStruct((rows, width), BF),
            ),
            in_specs=[SMEM] + [VMEM] * (4 + len(gram)),
            out_specs=(VMEM, VMEM),
            scratch_shapes=[pltpu.VMEM((2, 2 * width, naux), BF)],
            compiler_params=PARAMS,
        )(low, middle, left, right, factors, *gram)
        got = over(theirs, 1)
        new = pl.pallas_call(
            functools.partial(update_kernel, last),
            out_shape=jax.ShapeDtypeStruct((rows, width) if last else (width, rows), BF),
            in_specs=[SMEM] * 2 + [VMEM] * 5,
            out_specs=VMEM,
            compiler_params=PARAMS,
        )(occ_energy, pivot_energy, mine, got, coulomb_block, vir, vir_row)
        if not last:
            gram, middle = pl.pallas_call(
                gram_kernel,
                out_shape=(
                    jax.ShapeDtypeStruct((2, 2 * width, naux), F32),
                    jax.ShapeDtypeStruct((nocc, cols), F32),
                ),
                in_specs=[VMEM] * 5,
                out_specs=(VMEM, VMEM),
                scratch_shapes=[pltpu.VMEM((2 * width, rows), BF)],
                compiler_params=PARAMS,
            )(new, over(new, 1), left, right, factors)
            gram = all_reduce(*fold(gram, n_pair), n_pair)
    return new


def solution(mesh):
    in_specs = (
        P("pair", "aux"),
        P("pair", None),
        P("pair", "aux"),
        P("pair", "aux"),
        P("pair", "aux"),
        P("pair"),
        P(),
        P(),
    )
    out_specs = P("pair", "aux")
    return jax.shard_map(
        per_device, mesh=mesh, in_specs=in_specs, out_specs=out_specs, check_vma=False
    )
```

```python
import functools

import jax
import jax.numpy as jnp
from jax import lax
from jax.experimental import pallas as pl
from jax.experimental.pallas import tpu as pltpu
from jax.sharding import PartitionSpec as P

ITERS = 2
BF = jnp.bfloat16
F32 = jnp.float32
VMEM = pl.BlockSpec(memory_space=pltpu.VMEM)
SMEM = pl.BlockSpec(memory_space=pltpu.SMEM)
ANY = pl.BlockSpec(memory_space=pl.ANY)
FAR = lambda rows: [rows // 2, rows // 4, rows // 4]
DUE = {1: (0,), 3: (1,), 4: (2,)}
PARAMS = pltpu.CompilerParams(vmem_limit_bytes=12 * 2**20)


def xor(n, s):
    return [(i, i ^ s) for i in range(n)]


def dot(a, b, ca, cb):
    return lax.dot_general(a, b, (((ca,), (cb,)), ((), ())), preferred_element_type=F32)


def take(a, start, size, axis=0):
    return lax.dynamic_slice_in_dim(a, start, size, axis)


def tie(a, *others):
    return lax.optimization_barrier((a, *others))


def halves(v, low):
    half = v.shape[1] // 2
    return take(v, low * half, half, 1), take(v, (1 - low) * half, half, 1)


def fold(v, n):
    mine, theirs = halves(v, lax.axis_index("pair") % 2)
    return mine, lax.ppermute(theirs.astype(BF), "pair", xor(n, 1))


def all_reduce(mine, got, n, beside=lambda stage, a: a):
    high = lax.axis_index("pair") // 2
    m = n // 2
    part = mine.shape[1] // m

    def send(a, s):
        return lax.ppermute(a, "pair", xor(n, s))

    acc = mine + beside(0, got).astype(F32)
    rounded = acc.astype(BF)
    total = take(acc, high * part, part, 1)
    for s in range(1, m):
        total = total + send(take(rounded, (high ^ s) * part, part, 1), 2 * s).astype(F32)
    mine = beside(1, total.astype(BF))
    parts = [mine] + [send(mine, 2 * s) for s in range(1, m)]
    line = []
    for q in range(m):
        block = parts[0]
        for s in range(1, m):
            block = jnp.where((high ^ s) == q, parts[s], block)
        line.append(block)
    line = beside(2, jnp.concatenate(line, axis=1))
    return line, beside(3, send(line, 1))


def hold_kernel(own, far, out, sems):
    copies = [pltpu.make_async_copy(a, out.at[r], sems.at[r]) for r, a in enumerate((own, far))]
    for copy in copies:
        copy.start()
    for copy in copies:
        copy.wait()


def residual_kernel(swapped, side, middle, left, right, factors, one, two, mine, theirs, gram):
    nvirt, half, width = left.shape[0], one.shape[1], mine.shape[1]
    for j in range(2):
        rows = pl.ds(pl.multiple_of((side[0] if j == 0 else 1 - side[0]) * half, half), half)
        for r in range(2):
            gram[r, rows] = (one, two)[r][j] if swapped else (one, two)[j][r]
    size = min(nvirt, 256)
    for start in range(0, mine.shape[0], size):
        i, at = start // nvirt, start % nvirt
        if at == 0:
            scaled = (right[...].astype(F32) * middle[i : i + 1, :]).astype(BF)
        rows = slice(start, start + size)
        res = dot(left[at : at + size], scaled, 1, 1)
        for r in range(2):
            res += dot(factors[r, rows], gram[r], 1, 1)
        mine[rows] = res[:, :width]
        theirs[rows] = res[:, width:].astype(BF)


def update_kernel(last, occ, pivot, mine, got, coulomb, vir, vir_row, out):
    nvirt, width = vir.shape[1], mine.shape[1]
    virs = jnp.broadcast_to(vir[...], (width, nvirt)).T + vir_row[...]
    for i in range(mine.shape[0] // nvirt):
        rows = slice(i * nvirt, (i + 1) * nvirt)
        res = mine[rows] + got[rows].astype(F32)
        new = (coulomb[rows].astype(F32) + res) / (virs - occ[i] - pivot[0])
        if last:
            out[rows] = new.astype(BF)
        else:
            out[:, rows] = new.T.astype(BF)


def middle_kernel(mine, other, places, one, two, left, right, middle):
    width, nvirt = mine.shape[1], left.shape[0]
    part = one.shape[1]
    for a, at, column in ((one, places[0], places[1]), (two, 1 - places[0], 1 - places[1])):
        for top in range(2):
            left[pl.ds(pl.multiple_of(top * 2 * part + at * part, part), part)] = a[top]
        right[pl.ds(pl.multiple_of(column * part, part), part)] = a[2]
    for i in range(middle.shape[0]):
        total = None
        for at, amps in ((0, mine), (width, other)):
            proj = dot(amps[i * nvirt : (i + 1) * nvirt], left[...], 0, 0)
            term = jnp.sum(proj * right[at : at + width].astype(F32), axis=0, keepdims=True)
            total = term if total is None else total + term
        middle[i : i + 1] = total


def gram_kernel(mine, other, left, right, factors, gram, middle, amps):
    width, nvirt = mine.shape[0], left.shape[0]
    amps[:width] = mine[...]
    amps[width:] = other[...]
    for r in range(2):
        gram[r] = dot(amps[...], factors[r], 1, 0)
    for i in range(middle.shape[0]):
        proj = dot(amps[:, i * nvirt : (i + 1) * nvirt], left[...], 1, 0)
        middle[i : i + 1] = jnp.sum(proj * right[...].astype(F32), axis=0, keepdims=True)


def first_gram_kernel(mine, other, own, gram):
    width = mine.shape[1]
    gram[:width] = dot(mine[...], own[...], 0, 0)
    gram[width:] = dot(other[...], own[...], 0, 0)


def scheduled(micros):
    return pl.CostEstimate(flops=int(micros * 1e9), bytes_accessed=int(micros * 3e6), transcendentals=0)


def per_device(
    amplitudes, coulomb, df_factors, thc_left, thc_right, occ_energy, vir_energy, pivot_energy
):
    n_pair = lax.axis_size("pair")
    n_aux = lax.axis_size("aux")
    k = lax.axis_index("aux")
    me = lax.axis_index("pair")
    rows, width = amplitudes.shape
    nvirt = vir_energy.shape[0]
    nocc = rows // nvirt
    naux = df_factors.shape[1]
    low = (me % 2).reshape(1)

    def over(a, s):
        return lax.ppermute(a, "aux", xor(n_aux, s))

    fac = jnp.stack([thc_left, thc_right])
    fac = jnp.concatenate([fac, over(fac, 2)], axis=2)
    cols = fac.shape[-1]

    def other_rows(fac, axis):
        bit = n_pair >> (axis + 1)
        got = lax.ppermute(fac, "pair", xor(n_pair, bit))
        first = (me // bit) % 2 == 0
        return jnp.where(first, fac, got), jnp.where(first, got, fac)

    n_bits = n_pair.bit_length() - 1

    far_amps = over(amplitudes, 2)
    near = [amplitudes, over(amplitudes, 1)]

    def first_gram(pair_of):
        return pl.pallas_call(
            first_gram_kernel,
            out_shape=jax.ShapeDtypeStruct((2 * width, naux), F32),
            in_specs=[VMEM] * 3,
            out_specs=VMEM,
            compiler_params=PARAMS,
        )(*pair_of, df_factors)[None]

    near_mine, near_got = fold(first_gram(near), n_pair)
    far_amps, near_got, fac = tie(far_amps, near_got, fac)
    far_other, fac = tie(over(far_amps, 1), fac)
    far_gram = first_gram([far_amps, far_other])

    one, two = other_rows(fac, 0)
    kept = jnp.where(k // 2 == 0, one[1], two[1])
    fac = jnp.stack([one[0], two[0], kept])
    far_mine, far_got = fold(far_gram, n_pair)

    far = over(df_factors, 2)
    vir = vir_energy[None, :]
    vir_row = take(vir_energy, k * width, width)[None, :]
    coulomb_block = take(coulomb, k * width, width, 1)

    left = right = middle = factors = None

    def beside(stage, a):
        nonlocal fac, far, vir, vir_row, coulomb_block, left, right, middle, factors
        if stage == 1:
            a, fac = tie(a, fac)
        if stage == 2:
            fac = jnp.concatenate(other_rows(fac, n_bits - 1), axis=1)
            a, fac = tie(a, fac)
        if stage == 1:
            a, vir, vir_row, coulomb_block = tie(a, vir, vir_row, coulomb_block)
        if stage == 4:
            for axis in range(n_bits - 2, 1, -1):
                fac = jnp.concatenate(other_rows(fac, axis), axis=1)
            got = lax.ppermute(fac, "pair", xor(n_pair, n_pair // 4))
            bit = (me >> (n_bits - 2)) % 2
            left, right, middle = pl.pallas_call(
                middle_kernel,
                out_shape=(
                    jax.ShapeDtypeStruct((nvirt, cols), BF),
                    jax.ShapeDtypeStruct((2 * width, cols), BF),
                    jax.ShapeDtypeStruct((nocc, cols), F32),
                ),
                in_specs=[VMEM] * 2 + [SMEM] + [VMEM] * 2,
                out_specs=(VMEM,) * 3,
                cost_estimate=scheduled(3),
                compiler_params=PARAMS,
            )(*near, jnp.stack([bit, bit ^ (k % 2)]), fac, got)
        if stage == 4:
            factors = pl.pallas_call(
                hold_kernel,
                out_shape=jax.ShapeDtypeStruct((2, rows, naux), BF),
                in_specs=[ANY] * 2,
                out_specs=VMEM,
                scratch_shapes=[pltpu.SemaphoreType.DMA((2,))],
                compiler_params=PARAMS,
            )(df_factors, far)
            a, factors = tie(a, factors)
        return a

    line, other = all_reduce(
        jnp.concatenate([near_mine, far_mine], axis=0),
        jnp.concatenate([near_got, far_got], axis=0),
        n_pair,
        beside,
    )
    gram = (jnp.stack([line[0], other[0]]), beside(4, over(jnp.stack([line[1], other[1]]), 2)))
    for step in range(ITERS):
        last = step == ITERS - 1
        other = over(middle, 2)
        middle = middle + jnp.concatenate([other[:, cols // 2 :], other[:, : cols // 2]], axis=1)
        mine, theirs = pl.pallas_call(
            functools.partial(residual_kernel, step == 0),
            out_shape=(
                jax.ShapeDtypeStruct((rows, width), F32),
                jax.ShapeDtypeStruct((rows, width), BF),
            ),
            in_specs=[SMEM] + [VMEM] * (4 + len(gram)),
            out_specs=(VMEM, VMEM),
            scratch_shapes=[pltpu.VMEM((2, 2 * width, naux), BF)],
            compiler_params=PARAMS,
        )(low, middle, left, right, factors, *gram)
        got = over(theirs, 1)
        new = pl.pallas_call(
            functools.partial(update_kernel, last),
            out_shape=jax.ShapeDtypeStruct((rows, width) if last else (width, rows), BF),
            in_specs=[SMEM] * 2 + [VMEM] * 5,
            out_specs=VMEM,
            compiler_params=PARAMS,
        )(occ_energy, pivot_energy, mine, got, coulomb_block, vir, vir_row)
        if not last:
            gram, middle = pl.pallas_call(
                gram_kernel,
                out_shape=(
                    jax.ShapeDtypeStruct((2, 2 * width, naux), F32),
                    jax.ShapeDtypeStruct((nocc, cols), F32),
                ),
                in_specs=[VMEM] * 5,
                out_specs=(VMEM, VMEM),
                scratch_shapes=[pltpu.VMEM((2 * width, rows), BF)],
                compiler_params=PARAMS,
            )(new, over(new, 1), left, right, factors)
            gram = all_reduce(*fold(gram, n_pair), n_pair)
    return new


def solution(mesh):
    in_specs = (
        P("pair", "aux"),
        P("pair", None),
        P("pair", "aux"),
        P("pair", "aux"),
        P("pair", "aux"),
        P("pair"),
        P(),
        P(),
    )
    out_specs = P("pair", "aux")
    return jax.shard_map(
        per_device, mesh=mesh, in_specs=in_specs, out_specs=out_specs, check_vma=False
    )
```

```python
import functools

import jax
import jax.numpy as jnp
from jax import lax
from jax.experimental import pallas as pl
from jax.experimental.pallas import tpu as pltpu
from jax.sharding import PartitionSpec as P

ITERS = 2
BF = jnp.bfloat16
F32 = jnp.float32
VMEM = pl.BlockSpec(memory_space=pltpu.VMEM)
SMEM = pl.BlockSpec(memory_space=pltpu.SMEM)
ANY = pl.BlockSpec(memory_space=pl.ANY)
FAR = lambda rows: [rows // 2, rows // 4, rows // 4]
DUE = {1: (0,), 3: (1,), 4: (2,)}
PARAMS = pltpu.CompilerParams(vmem_limit_bytes=12 * 2**20)


def xor(n, s):
    return [(i, i ^ s) for i in range(n)]


def dot(a, b, ca, cb):
    return lax.dot_general(a, b, (((ca,), (cb,)), ((), ())), preferred_element_type=F32)


def take(a, start, size, axis=0):
    return lax.dynamic_slice_in_dim(a, start, size, axis)


def tie(a, *others):
    return lax.optimization_barrier((a, *others))


def halves(v, low):
    half = v.shape[1] // 2
    return take(v, low * half, half, 1), take(v, (1 - low) * half, half, 1)


def fold(v, n):
    mine, theirs = halves(v, lax.axis_index("pair") % 2)
    return mine, lax.ppermute(theirs.astype(BF), "pair", xor(n, 1))


def all_reduce(mine, got, n, beside=lambda stage, a: a):
    high = lax.axis_index("pair") // 2
    m = n // 2
    part = mine.shape[1] // m

    def send(a, s):
        return lax.ppermute(a, "pair", xor(n, s))

    acc = mine + beside(0, got).astype(F32)
    rounded = acc.astype(BF)
    total = take(acc, high * part, part, 1)
    for s in range(1, m):
        total = total + send(take(rounded, (high ^ s) * part, part, 1), 2 * s).astype(F32)
    mine = beside(1, total.astype(BF))
    parts = [mine] + [send(mine, 2 * s) for s in range(1, m)]
    line = []
    for q in range(m):
        block = parts[0]
        for s in range(1, m):
            block = jnp.where((high ^ s) == q, parts[s], block)
        line.append(block)
    line = beside(2, jnp.concatenate(line, axis=1))
    return line, beside(3, send(line, 1))


def hold_kernel(own, far, out, sems):
    copies = [pltpu.make_async_copy(a, out.at[r], sems.at[r]) for r, a in enumerate((own, far))]
    for copy in copies:
        copy.start()
    for copy in copies:
        copy.wait()


def residual_kernel(swapped, side, middle, left, right, factors, one, two, mine, theirs, gram):
    nvirt, half, width = left.shape[0], one.shape[1], mine.shape[1]
    for j in range(2):
        rows = pl.ds(pl.multiple_of((side[0] if j == 0 else 1 - side[0]) * half, half), half)
        for r in range(2):
            gram[r, rows] = (one, two)[r][j] if swapped else (one, two)[j][r]
    size = min(nvirt, 256)
    for start in range(0, mine.shape[0], size):
        i, at = start // nvirt, start % nvirt
        if at == 0:
            scaled = (right[...].astype(F32) * middle[i : i + 1, :]).astype(BF)
        rows = slice(start, start + size)
        res = dot(left[at : at + size], scaled, 1, 1)
        for r in range(2):
            res += dot(factors[r, rows], gram[r], 1, 1)
        mine[rows] = res[:, :width]
        theirs[rows] = res[:, width:].astype(BF)


def update_kernel(last, occ, pivot, mine, got, coulomb, vir, vir_row, out):
    nvirt, width = vir.shape[1], mine.shape[1]
    virs = jnp.broadcast_to(vir[...], (width, nvirt)).T + vir_row[...]
    for i in range(mine.shape[0] // nvirt):
        rows = slice(i * nvirt, (i + 1) * nvirt)
        res = mine[rows] + got[rows].astype(F32)
        new = (coulomb[rows].astype(F32) + res) / (virs - occ[i] - pivot[0])
        if last:
            out[rows] = new.astype(BF)
        else:
            out[:, rows] = new.T.astype(BF)


def middle_kernel(mine, other, places, one, two, left, right, middle):
    width, nvirt = mine.shape[1], left.shape[0]
    part = one.shape[1]
    for a, at, column in ((one, places[0], places[1]), (two, 1 - places[0], 1 - places[1])):
        for top in range(2):
            left[pl.ds(pl.multiple_of(top * 2 * part + at * part, part), part)] = a[top]
        right[pl.ds(pl.multiple_of(column * part, part), part)] = a[2]
    for i in range(middle.shape[0]):
        total = None
        for at, amps in ((0, mine), (width, other)):
            proj = dot(amps[i * nvirt : (i + 1) * nvirt], left[...], 0, 0)
            term = jnp.sum(proj * right[at : at + width].astype(F32), axis=0, keepdims=True)
            total = term if total is None else total + term
        middle[i : i + 1] = total


def gram_kernel(side, mine, other, left, right, factors, gram, *middle):
    width, nvirt = mine.shape[0], left.shape[0]
    for r, amps in enumerate((mine, other)):
        gram[0, r * width : (r + 1) * width] = dot(amps[...], factors[side], 1, 0)
    for out in middle:
        for i in range(out.shape[0]):
            total = None
            for r, amps in enumerate((mine, other)):
                proj = dot(amps[:, i * nvirt : (i + 1) * nvirt], left[...], 1, 0)
                term = proj * right[r * width : (r + 1) * width].astype(F32)
                total = term if total is None else total + term
            out[i : i + 1] = jnp.sum(total, axis=0, keepdims=True)


def first_gram_kernel(mine, other, own, gram):
    width = mine.shape[1]
    gram[:width] = dot(mine[...], own[...], 0, 0)
    gram[width:] = dot(other[...], own[...], 0, 0)


def scheduled(micros):
    return pl.CostEstimate(flops=int(micros * 1e9), bytes_accessed=int(micros * 3e6), transcendentals=0)


def per_device(
    amplitudes, coulomb, df_factors, thc_left, thc_right, occ_energy, vir_energy, pivot_energy
):
    n_pair = lax.axis_size("pair")
    n_aux = lax.axis_size("aux")
    k = lax.axis_index("aux")
    me = lax.axis_index("pair")
    rows, width = amplitudes.shape
    nvirt = vir_energy.shape[0]
    nocc = rows // nvirt
    naux = df_factors.shape[1]
    low = (me % 2).reshape(1)

    def over(a, s):
        return lax.ppermute(a, "aux", xor(n_aux, s))

    fac = jnp.stack([thc_left, thc_right])
    fac = jnp.concatenate([fac, over(fac, 2)], axis=2)
    cols = fac.shape[-1]

    def other_rows(fac, axis):
        bit = n_pair >> (axis + 1)
        got = lax.ppermute(fac, "pair", xor(n_pair, bit))
        first = (me // bit) % 2 == 0
        return jnp.where(first, fac, got), jnp.where(first, got, fac)

    n_bits = n_pair.bit_length() - 1

    far_amps = over(amplitudes, 2)
    near = [amplitudes, over(amplitudes, 1)]

    def first_gram(pair_of):
        return pl.pallas_call(
            first_gram_kernel,
            out_shape=jax.ShapeDtypeStruct((2 * width, naux), F32),
            in_specs=[VMEM] * 3,
            out_specs=VMEM,
            compiler_params=PARAMS,
        )(*pair_of, df_factors)[None]

    near_mine, near_got = fold(first_gram(near), n_pair)
    far_amps, near_got, fac = tie(far_amps, near_got, fac)
    far_other, fac = tie(over(far_amps, 1), fac)
    far_gram = first_gram([far_amps, far_other])

    one, two = other_rows(fac, 0)
    kept = jnp.where(k // 2 == 0, one[1], two[1])
    fac = jnp.stack([one[0], two[0], kept])
    far_mine, far_got = fold(far_gram, n_pair)

    far = over(df_factors, 2)
    vir = vir_energy[None, :]
    vir_row = take(vir_energy, k * width, width)[None, :]
    coulomb_block = take(coulomb, k * width, width, 1)

    left = right = middle = factors = None

    def beside(stage, a):
        nonlocal fac, far, vir, vir_row, coulomb_block, left, right, middle, factors
        if stage == 1:
            a, fac = tie(a, fac)
        if stage == 2:
            fac = jnp.concatenate(other_rows(fac, n_bits - 1), axis=1)
            a, fac = tie(a, fac)
        if stage == 1:
            a, vir, vir_row, coulomb_block = tie(a, vir, vir_row, coulomb_block)
        if stage == 4:
            for axis in range(n_bits - 2, 1, -1):
                fac = jnp.concatenate(other_rows(fac, axis), axis=1)
            got = lax.ppermute(fac, "pair", xor(n_pair, n_pair // 4))
            bit = (me >> (n_bits - 2)) % 2
            left, right, middle = pl.pallas_call(
                middle_kernel,
                out_shape=(
                    jax.ShapeDtypeStruct((nvirt, cols), BF),
                    jax.ShapeDtypeStruct((2 * width, cols), BF),
                    jax.ShapeDtypeStruct((nocc, cols), F32),
                ),
                in_specs=[VMEM] * 2 + [SMEM] + [VMEM] * 2,
                out_specs=(VMEM,) * 3,
                cost_estimate=scheduled(3),
                compiler_params=PARAMS,
            )(*near, jnp.stack([bit, bit ^ (k % 2)]), fac, got)
        if stage == 4:
            factors = pl.pallas_call(
                hold_kernel,
                out_shape=jax.ShapeDtypeStruct((2, rows, naux), BF),
                in_specs=[ANY] * 2,
                out_specs=VMEM,
                scratch_shapes=[pltpu.SemaphoreType.DMA((2,))],
                compiler_params=PARAMS,
            )(df_factors, far)
            a, factors = tie(a, factors)
        return a

    line, other = all_reduce(
        jnp.concatenate([near_mine, far_mine], axis=0),
        jnp.concatenate([near_got, far_got], axis=0),
        n_pair,
        beside,
    )
    gram = (jnp.stack([line[0], other[0]]), beside(4, over(jnp.stack([line[1], other[1]]), 2)))
    for step in range(ITERS):
        last = step == ITERS - 1
        other = over(middle, 2)
        middle = middle + jnp.concatenate([other[:, cols // 2 :], other[:, : cols // 2]], axis=1)
        mine, theirs = pl.pallas_call(
            functools.partial(residual_kernel, step == 0),
            out_shape=(
                jax.ShapeDtypeStruct((rows, width), F32),
                jax.ShapeDtypeStruct((rows, width), BF),
            ),
            in_specs=[SMEM] + [VMEM] * (4 + len(gram)),
            out_specs=(VMEM, VMEM),
            scratch_shapes=[pltpu.VMEM((2, 2 * width, naux), BF)],
            compiler_params=PARAMS,
        )(low, middle, left, right, factors, *gram)
        got = over(theirs, 1)
        new = pl.pallas_call(
            functools.partial(update_kernel, last),
            out_shape=jax.ShapeDtypeStruct((rows, width) if last else (width, rows), BF),
            in_specs=[SMEM] * 2 + [VMEM] * 5,
            out_specs=VMEM,
            compiler_params=PARAMS,
        )(occ_energy, pivot_energy, mine, got, coulomb_block, vir, vir_row)
        if not last:
            amps = (new, over(new, 1))
            folded = []
            for side in range(2):
                shape = (jax.ShapeDtypeStruct((1, 2 * width, naux), F32),)
                if side:
                    shape += (jax.ShapeDtypeStruct((nocc, cols), F32),)
                terms = pl.pallas_call(
                    functools.partial(gram_kernel, side),
                    out_shape=shape,
                    in_specs=[VMEM] * 5,
                    out_specs=(VMEM,) * len(shape),
                    compiler_params=PARAMS,
                )(*amps, left, right, factors)
                folded.append(fold(terms[0], n_pair))
            middle = terms[1]
            gram = all_reduce(*(jnp.concatenate(a, axis=0) for a in zip(*folded)), n_pair)
    return new


def solution(mesh):
    in_specs = (
        P("pair", "aux"),
        P("pair", None),
        P("pair", "aux"),
        P("pair", "aux"),
        P("pair", "aux"),
        P("pair"),
        P(),
        P(),
    )
    out_specs = P("pair", "aux")
    return jax.shard_map(
        per_device, mesh=mesh, in_specs=in_specs, out_specs=out_specs, check_vma=False
    )
```

```python
import functools

import jax
import jax.numpy as jnp
from jax import lax
from jax.experimental import pallas as pl
from jax.experimental.pallas import tpu as pltpu
from jax.sharding import PartitionSpec as P

ITERS = 2
BF = jnp.bfloat16
F32 = jnp.float32
VMEM = pl.BlockSpec(memory_space=pltpu.VMEM)
SMEM = pl.BlockSpec(memory_space=pltpu.SMEM)
ANY = pl.BlockSpec(memory_space=pl.ANY)
FAR = lambda rows: [rows // 2, rows // 4, rows // 4]
DUE = {1: (0,), 3: (1,), 4: (2,)}
PARAMS = pltpu.CompilerParams(vmem_limit_bytes=12 * 2**20)


def xor(n, s):
    return [(i, i ^ s) for i in range(n)]


def dot(a, b, ca, cb):
    return lax.dot_general(a, b, (((ca,), (cb,)), ((), ())), preferred_element_type=F32)


def take(a, start, size, axis=0):
    return lax.dynamic_slice_in_dim(a, start, size, axis)


def tie(a, *others):
    return lax.optimization_barrier((a, *others))


def halves(v, low):
    half = v.shape[1] // 2
    return take(v, low * half, half, 1), take(v, (1 - low) * half, half, 1)


def fold(v, n):
    mine, theirs = halves(v, lax.axis_index("pair") % 2)
    return mine, lax.ppermute(theirs.astype(BF), "pair", xor(n, 1))


def all_reduce(mine, got, n, beside=lambda stage, a: a):
    high = lax.axis_index("pair") // 2
    m = n // 2
    part = mine.shape[1] // m

    def send(a, s):
        return lax.ppermute(a, "pair", xor(n, s))

    acc = mine + beside(0, got).astype(F32)
    rounded = acc.astype(BF)
    total = take(acc, high * part, part, 1)
    for s in range(1, m):
        total = total + send(take(rounded, (high ^ s) * part, part, 1), 2 * s).astype(F32)
    mine = beside(1, total.astype(BF))
    parts = [mine] + [send(mine, 2 * s) for s in range(1, m)]
    line = []
    for q in range(m):
        block = parts[0]
        for s in range(1, m):
            block = jnp.where((high ^ s) == q, parts[s], block)
        line.append(block)
    line = beside(2, jnp.concatenate(line, axis=1))
    return line, beside(3, send(line, 1))


def hold_kernel(own, far, out, sems):
    copies = [pltpu.make_async_copy(a, out.at[r], sems.at[r]) for r, a in enumerate((own, far))]
    for copy in copies:
        copy.start()
    for copy in copies:
        copy.wait()


def residual_kernel(swapped, side, middle, left, right, factors, one, two, mine, theirs, gram):
    nvirt, half, width = left.shape[0], one.shape[1], mine.shape[1]
    for j in range(2):
        rows = pl.ds(pl.multiple_of((side[0] if j == 0 else 1 - side[0]) * half, half), half)
        for r in range(2):
            gram[r, rows] = (one, two)[r][j] if swapped else (one, two)[j][r]
    size = min(nvirt, 256)
    for start in range(0, mine.shape[0], size):
        i, at = start // nvirt, start % nvirt
        if at == 0:
            scaled = (right[...].astype(F32) * middle[i : i + 1, :]).astype(BF)
        rows = slice(start, start + size)
        res = dot(left[at : at + size], scaled, 1, 1)
        for r in range(2):
            res += dot(factors[r, rows], gram[r], 1, 1)
        mine[rows] = res[:, :width]
        theirs[rows] = res[:, width:].astype(BF)


def update_kernel(last, occ, pivot, mine, got, coulomb, vir, vir_row, out):
    nvirt, width = vir.shape[1], mine.shape[1]
    virs = jnp.broadcast_to(vir[...], (width, nvirt)).T + vir_row[...]
    for i in range(mine.shape[0] // nvirt):
        rows = slice(i * nvirt, (i + 1) * nvirt)
        res = mine[rows] + got[rows].astype(F32)
        new = (coulomb[rows].astype(F32) + res) / (virs - occ[i] - pivot[0])
        if last:
            out[rows] = new.astype(BF)
        else:
            out[:, rows] = new.T.astype(BF)


def middle_kernel(mine, other, places, one, two, left, right, middle):
    width, nvirt = mine.shape[1], left.shape[0]
    part = one.shape[1]
    for a, at, column in ((one, places[0], places[1]), (two, 1 - places[0], 1 - places[1])):
        for top in range(2):
            left[pl.ds(pl.multiple_of(top * 2 * part + at * part, part), part)] = a[top]
        right[pl.ds(pl.multiple_of(column * part, part), part)] = a[2]
    for i in range(middle.shape[0]):
        total = None
        for at, amps in ((0, mine), (width, other)):
            proj = dot(amps[i * nvirt : (i + 1) * nvirt], left[...], 0, 0)
            term = jnp.sum(proj * right[at : at + width].astype(F32), axis=0, keepdims=True)
            total = term if total is None else total + term
        middle[i : i + 1] = total


def gram_kernel(side, mine, other, left, right, factors, gram, *middle):
    width, nvirt = mine.shape[0], left.shape[0]
    for r, amps in enumerate((mine, other)):
        gram[0, r * width : (r + 1) * width] = dot(amps[...], factors[side], 1, 0)
    for out in middle:
        for i in range(out.shape[0]):
            total = None
            for r, amps in enumerate((mine, other)):
                proj = dot(amps[:, i * nvirt : (i + 1) * nvirt], left[...], 1, 0)
                term = proj * right[r * width : (r + 1) * width].astype(F32)
                total = term if total is None else total + term
            out[i : i + 1] = jnp.sum(total, axis=0, keepdims=True)


def first_gram_kernel(mine, other, own, gram):
    width = mine.shape[1]
    gram[:width] = dot(mine[...], own[...], 0, 0)
    gram[width:] = dot(other[...], own[...], 0, 0)


def scheduled(micros):
    return pl.CostEstimate(flops=int(micros * 1e9), bytes_accessed=int(micros * 3e6), transcendentals=0)


def per_device(
    amplitudes, coulomb, df_factors, thc_left, thc_right, occ_energy, vir_energy, pivot_energy
):
    n_pair = lax.axis_size("pair")
    n_aux = lax.axis_size("aux")
    k = lax.axis_index("aux")
    me = lax.axis_index("pair")
    rows, width = amplitudes.shape
    nvirt = vir_energy.shape[0]
    nocc = rows // nvirt
    naux = df_factors.shape[1]
    low = (me % 2).reshape(1)

    def over(a, s):
        return lax.ppermute(a, "aux", xor(n_aux, s))

    fac = jnp.stack([thc_left, thc_right])
    fac = jnp.concatenate([fac, over(fac, 2)], axis=2)
    cols = fac.shape[-1]

    def other_rows(fac, axis):
        bit = n_pair >> (axis + 1)
        got = lax.ppermute(fac, "pair", xor(n_pair, bit))
        first = (me // bit) % 2 == 0
        return jnp.where(first, fac, got), jnp.where(first, got, fac)

    n_bits = n_pair.bit_length() - 1

    far_amps = over(amplitudes, 2)
    near = [amplitudes, over(amplitudes, 1)]

    def first_gram(pair_of):
        return pl.pallas_call(
            first_gram_kernel,
            out_shape=jax.ShapeDtypeStruct((2 * width, naux), F32),
            in_specs=[VMEM] * 3,
            out_specs=VMEM,
            compiler_params=PARAMS,
        )(*pair_of, df_factors)[None]

    near_mine, near_got = fold(first_gram(near), n_pair)
    far_amps, near_got, fac = tie(far_amps, near_got, fac)
    far_other, fac = tie(over(far_amps, 1), fac)
    far_gram = first_gram([far_amps, far_other])

    one, two = other_rows(fac, 0)
    kept = jnp.where(k // 2 == 0, one[1], two[1])
    fac = jnp.stack([one[0], two[0], kept])
    far_mine, far_got = fold(far_gram, n_pair)

    far = over(df_factors, 2)
    vir = vir_energy[None, :]
    vir_row = take(vir_energy, k * width, width)[None, :]
    coulomb_block = take(coulomb, k * width, width, 1)

    left = right = middle = factors = None

    def beside(stage, a):
        nonlocal fac, far, vir, vir_row, coulomb_block, left, right, middle, factors
        if stage == 1:
            a, fac = tie(a, fac)
        if stage == 2:
            fac = jnp.concatenate(other_rows(fac, n_bits - 1), axis=1)
            a, fac = tie(a, fac)
        if stage == 1:
            a, vir, vir_row, coulomb_block = tie(a, vir, vir_row, coulomb_block)
        if stage == 4:
            for axis in range(n_bits - 2, 1, -1):
                fac = jnp.concatenate(other_rows(fac, axis), axis=1)
            got = lax.ppermute(fac, "pair", xor(n_pair, n_pair // 4))
            bit = (me >> (n_bits - 2)) % 2
            left, right, middle = pl.pallas_call(
                middle_kernel,
                out_shape=(
                    jax.ShapeDtypeStruct((nvirt, cols), BF),
                    jax.ShapeDtypeStruct((2 * width, cols), BF),
                    jax.ShapeDtypeStruct((nocc, cols), F32),
                ),
                in_specs=[VMEM] * 2 + [SMEM] + [VMEM] * 2,
                out_specs=(VMEM,) * 3,
                cost_estimate=scheduled(3),
                compiler_params=PARAMS,
            )(*near, jnp.stack([bit, bit ^ (k % 2)]), fac, got)
        if stage == 4:
            factors = pl.pallas_call(
                hold_kernel,
                out_shape=jax.ShapeDtypeStruct((2, rows, naux), BF),
                in_specs=[ANY] * 2,
                out_specs=VMEM,
                scratch_shapes=[pltpu.SemaphoreType.DMA((2,))],
                compiler_params=PARAMS,
            )(df_factors, far)
            a, factors = tie(a, factors)
        return a

    line, other = all_reduce(
        jnp.concatenate([near_mine, far_mine], axis=0),
        jnp.concatenate([near_got, far_got], axis=0),
        n_pair,
        beside,
    )
    gram = (jnp.stack([line[0], other[0]]), beside(4, over(jnp.stack([line[1], other[1]]), 2)))
    for step in range(ITERS):
        last = step == ITERS - 1
        other = over(middle, 2) if step == 0 else crossed[0]
        middle = middle + jnp.concatenate([other[:, cols // 2 :], other[:, : cols // 2]], axis=1)
        mine, theirs = pl.pallas_call(
            functools.partial(residual_kernel, step == 0),
            out_shape=(
                jax.ShapeDtypeStruct((rows, width), F32),
                jax.ShapeDtypeStruct((rows, width), BF),
            ),
            in_specs=[SMEM] + [VMEM] * (4 + len(gram)),
            out_specs=(VMEM, VMEM),
            scratch_shapes=[pltpu.VMEM((2, 2 * width, naux), BF)],
            compiler_params=PARAMS,
        )(low, middle, left, right, factors, *gram)
        got = over(theirs, 1)
        new = pl.pallas_call(
            functools.partial(update_kernel, last),
            out_shape=jax.ShapeDtypeStruct((rows, width) if last else (width, rows), BF),
            in_specs=[SMEM] * 2 + [VMEM] * 5,
            out_specs=VMEM,
            compiler_params=PARAMS,
        )(occ_energy, pivot_energy, mine, got, coulomb_block, vir, vir_row)
        if not last:
            amps = (new, over(new, 1))
            folded = []
            for side in range(2):
                shape = (jax.ShapeDtypeStruct((1, 2 * width, naux), F32),)
                if side:
                    shape += (jax.ShapeDtypeStruct((nocc, cols), F32),)
                terms = pl.pallas_call(
                    functools.partial(gram_kernel, side),
                    out_shape=shape,
                    in_specs=[VMEM] * 5,
                    out_specs=(VMEM,) * len(shape),
                    compiler_params=PARAMS,
                )(*amps, left, right, factors)
                folded.append(fold(terms[0], n_pair))
            middle = terms[1]
            crossed = [over(middle, 2)]

            def with_middle(stage, a):
                if stage == 0:
                    a, crossed[0] = tie(a, crossed[0])
                return a

            gram = all_reduce(*(jnp.concatenate(a, axis=0) for a in zip(*folded)), n_pair, with_middle)
    return new


def solution(mesh):
    in_specs = (
        P("pair", "aux"),
        P("pair", None),
        P("pair", "aux"),
        P("pair", "aux"),
        P("pair", "aux"),
        P("pair"),
        P(),
        P(),
    )
    out_specs = P("pair", "aux")
    return jax.shard_map(
        per_device, mesh=mesh, in_specs=in_specs, out_specs=out_specs, check_vma=False
    )
```
